512 devices in a mesh: seq: 128 (over z, y, core), hid: 4 (over x).
Axes of the slice: x: 4, y: 4, z: 16, core: 2. Of those that a mesh axis runs over, the one named last changes fastest.
Arguments:
- glu: bfloat16 [16384, 1024], P('seq', 'hid'), may hold values from -6 to 6
- dw_kernel: float32 [31, 1024], P(None, 'hid'), may hold values from -1 to 1
- bn_scale: float32 [1024], P('hid'), may hold values from 0.5 to 2
- bn_shift: float32 [1024], P('hid'), may hold values from -3 to 3
- pw_out: bfloat16 [1024, 1024], P('hid'), may hold values from -0.1875 to 0.1875
- block_input: bfloat16 [16384, 1024], P('seq'), may hold values from -6 to 6
- ln_gain: float32 [1024], replicated, may hold values from 0.5 to 2
- w_up: bfloat16 [128, 1024, 4096], P('seq', None, 'hid'), may hold values from -0.1875 to 0.1875
- w_down: bfloat16 [128, 4096, 1024], P('seq', 'hid'), may hold values from -0.09375 to 0.09375
- routes: int32 [16384, 2], P('seq'), may hold values from 0 to 127, all different within a row; in each aligned block of 128 rows (0 to 127, 128 to 255, ...) at most 6 rows name the same one
- gates: float32 [16384, 2], P('seq'), may hold values from 0.2 to 1
Outputs:
- block_output: bfloat16 [16384, 1024], P('seq', 'hid')
The draws below stay inside these ranges and needn't reach their ends.
Inputs may be any that keep to these rules, and one draw needn't show every extreme that they name: `routes`: each frame names 2 different experts. Among the frames of one index of seq (aligned blocks of 128 frames) no expert is named more than 6 times, a bound that some block reaches.
All inputs are finite; a program needn't handle non-finite values.
Results may differ from the reference program's by a relative error of at most 0.011.
Values may be sent and summed in bfloat16 or wider, within the bound.
No kernel may reach another device: no remote copies, remote signals or barrier semaphores. Data moves between devices by JAX's collectives and lax.ppermute only.
A program may use at most 64 MiB of HBM per device.

```python
import math
import jax
import jax.numpy as jnp
import numpy as np
from jax import lax

D = 1024
FF = 4096
KER = 31
TOP = 2
TOK_DEV = 128
FRAMES = 16384
EXPERTS = 128
CAP = 6
N_SEQ = 128


def shard_levels(rng, extent, shards, low, largest):
    factor_of, own = 1.0, jax.random.fold_in(rng, 6)
    for dim, shards_of in shards:
        steps = jnp.exp(jax.random.uniform(jax.random.fold_in(own, dim), (shards_of,), jnp.float32, low / len(shards), largest / len(shards)))
        factor_of = factor_of * jnp.repeat(steps, extent[dim] // shards_of).reshape([-1 if axis == dim else 1 for axis in range(len(extent))])
    return factor_of


def routed_block(key, own, number, rows, number_of, top, reach, lean):
    sequence = jax.random.permutation(key, number_of)
    crowded, ordinary = portions_of(number_of, rows * top, reach, lean, True), portions_of(number_of, rows * top, reach, lean, False)
    places = jnp.arange(number_of)

    def named(tallies, turn):
        used = int((tallies > 0).sum())
        fixed = max(1, used // 4)
        shifted = fixed + (places - fixed + turn * (used - fixed)) % max(1, number_of - fixed)
        return jnp.zeros((number_of,), jnp.int32).at[sequence[jnp.where(places < fixed, places, shifted)]].set(jnp.asarray(tallies, jnp.int32))

    tallies = jnp.where(number % 4 == 0, named(crowded, number // 4), named(ordinary, number - number // 4 - 1))
    mixed = jax.random.permutation(jax.random.fold_in(own, 3), number_of)
    source_of, receiver = mixed[0:number_of // 2 * 2:2], mixed[1:number_of // 2 * 2:2]
    margin = jnp.minimum(tallies[source_of] - 1, reach - tallies[receiver]) // 2
    margin = jnp.where((source_of == sequence[0]) | (receiver == sequence[0]) | (tallies[receiver] == 0), 0, jnp.maximum(margin, 0))
    shifted = jax.random.randint(jax.random.fold_in(own, 4), (number_of // 2,), 0, 1 << 20) % (margin + 1)
    tallies = tallies.at[source_of].add(-shifted).at[receiver].add(shifted)
    members = jnp.searchsorted(jnp.cumsum(tallies), jnp.arange(rows * top), side="right").astype(jnp.int32)
    grid = members.reshape(top, rows).T
    grid = grid[jax.random.permutation(jax.random.fold_in(own, 1), rows)]
    turn = jax.random.randint(jax.random.fold_in(own, 2), (rows, 1), 0, top)
    return jnp.take_along_axis(grid, (jnp.arange(top)[None, :] + turn) % top, axis=1)


def portions_of(number_of, total, bound, slope, full):
    weights = [(1 << 20) // math.isqrt(standing ** slope) + 1 for standing in range(1, number_of + 1)]
    largest = bound if full else min(bound, max(-(-total // number_of), total * weights[0] // sum(weights)))
    least = 1 if total - largest >= number_of - 1 else 0
    holding, surplus = [largest] + [least] * (number_of - 1), total - largest - least * (number_of - 1)
    while surplus > 0:
        movable = [i for i in range(1, number_of) if holding[i] < largest] or [i for i in range(1, number_of) if holding[i] < bound]
        pool, budget = sum([weights[i] for i in movable]), surplus
        for i in movable:
            extra = min(bound - holding[i], max(1, budget * weights[i] // pool), surplus)
            holding[i] = holding[i] + extra
            surplus = surplus - extra
    return np.array(holding)


def gaussian(own_key, shape, width, bound, pieces=(), held_as=jnp.bfloat16):
    entries = jax.random.normal(own_key, shape, jnp.float32) * width
    if len(pieces) > 0:
        entries = shard_levels(own_key, shape, pieces, -0.22, 0.18) * entries
    return jnp.clip(entries, min=-bound, max=bound).astype(held_as)


def setup_inputs(seed: int = 0) -> dict:
    arg_keys = jax.random.split(jax.random.key(seed), 12)
    glu = gaussian(arg_keys[0], (FRAMES, D), 1.0, 6.0, ((0, 128), (1, 4)))
    dw_kernel = gaussian(arg_keys[1], (KER, D), KER ** -0.5, 1.0, ((1, 4),), jnp.float32)
    bn_scale = jnp.clip(jnp.exp(math.log(2.0) - 1.3862944 * jax.random.uniform(arg_keys[2], (D,), jnp.float32) ** shard_levels(arg_keys[2], (D,), ((0, 4),), -0.2, 0.2)), 0.5, 2.0)
    bn_shift = gaussian(arg_keys[3], (D,), 0.5, 3.0, ((0, 4),), jnp.float32)
    pw_out = gaussian(arg_keys[4], (D, D), D ** -0.5, 0.1875, ((0, 4),))
    block_input = gaussian(arg_keys[5], (FRAMES, D), 1.0, 6.0, ((0, 128),))
    ln_gain = jnp.clip(jnp.exp(jax.random.uniform(arg_keys[6], (D,), jnp.float32, math.log(0.5), math.log(2.0))), 0.5, 2.0)
    w_up = gaussian(arg_keys[7], (EXPERTS, D, FF), D ** -0.5, 0.1875, ((0, 128), (2, 4)))
    w_down = gaussian(arg_keys[8], (EXPERTS, FF, D), FF ** -0.5, 0.09375, ((0, 128), (1, 4)))
    routes_keys = jax.random.split(jax.random.fold_in(arg_keys[9], 1), FRAMES // TOK_DEV)
    routes_turns = jax.random.permutation(jax.random.fold_in(arg_keys[9], 3), FRAMES // TOK_DEV)
    routes = jax.vmap(lambda own, number: routed_block(jax.random.fold_in(arg_keys[9], 2), own, number, TOK_DEV, EXPERTS, TOP, CAP, 2))(routes_keys, routes_turns).reshape((FRAMES, TOP))
    gates = jnp.clip(0.2 + 0.8 * jax.random.uniform(arg_keys[10], (FRAMES, TOP), jnp.float32) ** shard_levels(arg_keys[10], (FRAMES, TOP), ((0, 128),), -0.2, 0.2), 0.2, 1.0)
    return {"glu": glu, "dw_kernel": dw_kernel, "bn_scale": bn_scale, "bn_shift": bn_shift, "pw_out": pw_out, "block_input": block_input, "ln_gain": ln_gain, "w_up": w_up, "w_down": w_down, "routes": routes, "gates": gates}


def reference(glu, dw_kernel, bn_scale, bn_shift, pw_out, block_input, ln_gain, w_up, w_down, routes, gates):
    frames = glu.shape[0]
    half_span = KER // 2
    padded = jnp.pad(glu.astype(jnp.float32), ((half_span, half_span), (0, 0)))
    depth_sum = jnp.zeros((frames, D), jnp.float32)
    for offset in range(KER):
        depth_sum = depth_sum + padded[offset:offset + frames] * dw_kernel[offset]
    activated = jax.nn.silu(depth_sum * bn_scale + bn_shift).astype(jnp.bfloat16)
    mixed = block_input.astype(jnp.float32) + jnp.dot(activated, pw_out, preferred_element_type=jnp.float32)
    average = lax.optimization_barrier(jnp.mean(mixed, axis=1, keepdims=True))
    centered = mixed - average
    spread = lax.optimization_barrier(jnp.mean(centered * centered, axis=1, keepdims=True))
    normed = (centered / jnp.sqrt(spread + 1e-05) * ln_gain).astype(jnp.bfloat16)
    blocks = routes.reshape(N_SEQ, TOP * TOK_DEV)
    onehot = (blocks[:, :, None] == jnp.arange(EXPERTS, dtype=jnp.int32)[None, None, :]).astype(jnp.int32)
    position = lax.optimization_barrier(jnp.sum(jnp.cumsum(onehot, axis=1) * onehot, axis=2)) - 1
    source = jnp.arange(N_SEQ, dtype=jnp.int32)[:, None]
    slot_index = ((blocks * N_SEQ + source) * CAP + position).reshape(-1).astype(jnp.int32)
    buffer = jnp.zeros((EXPERTS * N_SEQ * CAP, D), jnp.bfloat16)
    buffer = buffer.at[slot_index].set(jnp.repeat(normed, TOP, axis=0))

    def expert_pass(items):
        rows, up_proj, down_proj = items
        hidden = jax.nn.silu(jnp.dot(rows, up_proj, preferred_element_type=jnp.float32)).astype(jnp.bfloat16)
        return jnp.dot(hidden, down_proj, preferred_element_type=jnp.float32).astype(jnp.bfloat16)
    outputs = lax.map(expert_pass, (buffer.reshape(EXPERTS, N_SEQ * CAP, D), w_up, w_down)).reshape(-1, D)
    picked = outputs[slot_index].astype(jnp.float32).reshape(frames, TOP, D)
    moe = lax.optimization_barrier(jnp.sum(picked * gates[:, :, None], axis=1))
    return (mixed + moe).astype(jnp.bfloat16)
```

```python
import functools

import jax
import jax.numpy as jnp
from jax import lax
from jax.experimental import pallas as pl
from jax.experimental.pallas import tpu as pltpu
from jax.sharding import Mesh, PartitionSpec as P

Z, Y, C, X = 16, 4, 2, 4
YC = Y * C
ROWS = 128
QUARTER = 256
WIDTH = 1024
TAPS = 31
CAP = 6
EDGE = 16
SLOTS = Z * CAP * YC
BLOCK = Z * CAP
AUX = 8

F32, BF16 = jnp.float32, jnp.bfloat16


def dot(a, b, dims=((1,), (0,))):
    return lax.dot_general(a, b, (dims, ((), ())), preferred_element_type=F32)


def silu(v):
    return v / (1.0 + jnp.exp(-v))


def cost(flops, nbytes):
    return pl.CostEstimate(flops=flops, bytes_accessed=nbytes, transcendentals=0)


def call(body, out_shape, name, flops=10**6, nbytes=10**6, scratch=(), vmem=32 << 20, smem=()):
    def run(*args):
        in_specs = [
            pl.BlockSpec(memory_space=pltpu.SMEM if i in smem else pltpu.VMEM)
            for i in range(len(args))
        ]
        return pl.pallas_call(
            body,
            out_shape=out_shape,
            in_specs=in_specs,
            out_specs=jax.tree.map(lambda _: pl.BlockSpec(memory_space=pltpu.VMEM), out_shape),
            scratch_shapes=list(scratch),
            cost_estimate=cost(flops, nbytes),
            compiler_params=pltpu.CompilerParams(vmem_limit_bytes=vmem),
            name=name,
        )(*args)

    return run


def shape(dims, dtype):
    return jax.ShapeDtypeStruct(dims, dtype)


def lanes_to_rows(row):
    return jnp.transpose(jnp.broadcast_to(row, (ROWS, ROWS)))


def routing_kernel(routes_ref, gates_ref, put_ref, pick_ref, gate_ref):
    routes = routes_ref[...]
    expert = lax.broadcasted_iota(jnp.int32, (ROWS, ROWS), 0)
    frame = lax.broadcasted_iota(jnp.int32, (ROWS, ROWS), 1)
    before = (expert < frame).astype(F32).astype(BF16)
    chosen = [(expert == routes[j : j + 1]).astype(F32) for j in range(2)]
    earlier = dot((chosen[0] + chosen[1]).astype(BF16), before)
    slot_row = lax.broadcasted_iota(jnp.int32, (SLOTS, ROWS), 0)
    slot_lane = lax.broadcasted_iota(jnp.int32, (ROWS, SLOTS), 1)
    put = None
    for j in range(2):
        position = jnp.sum(chosen[j] * earlier, axis=0, keepdims=True).astype(jnp.int32)
        named = routes[j : j + 1]
        slot = (named // YC) * (CAP * YC) + position * YC + named % YC
        here = slot_row == slot
        put = here if put is None else put | here
        slot_col = lanes_to_rows(slot.astype(F32))[:, 0:1].astype(jnp.int32)
        pick_ref[j] = (slot_lane == slot_col).astype(F32).astype(BF16)
        gate_ref[j] = lanes_to_rows(gates_ref[j : j + 1])
    put_ref[...] = put.astype(F32).astype(BF16)


def own_conv_kernel(glu_ref, taps_ref, out_ref, padded):
    padded[0:EDGE] = jnp.zeros((EDGE, QUARTER), F32)
    padded[EDGE + ROWS :] = jnp.zeros((EDGE, QUARTER), F32)
    padded[EDGE : EDGE + ROWS] = glu_ref[...].astype(F32)
    total = None
    for k in range(TAPS):
        term = padded[k + 1 : k + 1 + ROWS] * taps_ref[k : k + 1]
        total = term if total is None else total + term
    out_ref[...] = total


def front_kernel(
    own_ref, low_ref, high_ref, taps_ref, scale_ref, shift_ref, pw_ref, input_ref, out_ref, low, high, depth
):
    low[0:EDGE] = low_ref[...].astype(F32)
    low[EDGE:] = jnp.zeros((2 * EDGE, QUARTER), F32)
    high[0 : 2 * EDGE] = jnp.zeros((2 * EDGE, QUARTER), F32)
    high[2 * EDGE :] = high_ref[...].astype(F32)
    depth[...] = own_ref[...]
    first, last = depth[0:EDGE], depth[ROWS - EDGE :]
    for k in range(TAPS):
        tap = taps_ref[k : k + 1]
        first = first + low[k + 1 : k + 1 + EDGE] * tap
        last = last + high[k + 1 : k + 1 + EDGE] * tap
    depth[0:EDGE] = first
    depth[ROWS - EDGE :] = last
    activated = silu(depth[...] * scale_ref[...] + shift_ref[...]).astype(BF16)
    row_sum = 0.25 * jnp.sum(input_ref[...].astype(F32), axis=1, keepdims=True)
    for x in range(X):
        part = dot(activated, pw_ref[:, x * QUARTER : (x + 1) * QUARTER])
        out_ref[x, 0:ROWS] = part
        row_sum = row_sum + jnp.sum(part, axis=1, keepdims=True)
    sums = jnp.transpose(jnp.broadcast_to(row_sum, (ROWS, ROWS)))
    for x in range(X):
        out_ref[x, ROWS:] = jnp.concatenate([sums[0:AUX], sums[0:AUX]], axis=1)


def dispatch_kernel(x_ref, parts_ref, input_ref, gain_ref, put_ref, mixed_ref, out_ref):
    columns = pl.ds(pl.multiple_of(x_ref[0] * QUARTER, QUARTER), QUARTER)
    mixed = input_ref[:, columns].astype(F32)
    sums = jnp.zeros((AUX, ROWS), F32)
    for x in range(X):
        mixed = mixed + parts_ref[x, 0:ROWS]
        sums = sums + parts_ref[x, ROWS:, 0:ROWS]
    mean = lanes_to_rows(sums[0:1])[:, 0:1] * (1.0 / WIDTH)
    mixed_ref[...] = mixed
    scaled = ((mixed - mean) * gain_ref[:, columns]).astype(BF16)
    out_ref[...] = dot(put_ref[...], scaled).astype(BF16)


def spread_kernel(in_ref, out_ref, wide):
    for half in range(2):
        lanes = slice(half * 128, (half + 1) * 128)
        wide[half] = in_ref[:, lanes].astype(F32)
        for yc in range(YC):
            block = wide[half, pl.ds(yc, BLOCK, stride=YC)].astype(BF16)
            for x in range(X):
                out_ref[yc, x, :, lanes] = block


def expert_kernel(in_ref, gain_ref, up_ref, down_ref, out_ref):
    blocks = in_ref.shape[0]
    rows = jnp.concatenate(
        [in_ref[:, x].reshape(blocks * BLOCK, QUARTER) for x in range(X)], axis=1
    )
    centered = rows.astype(F32) / gain_ref[...]
    spread = jnp.sum(centered * centered, axis=1, keepdims=True) * (1.0 / WIDTH)
    inverse = 1.0 / jnp.sqrt(spread + 1e-05)
    hidden = silu(dot(rows, up_ref[...]) * inverse).astype(BF16)
    result = dot(hidden, down_ref[...]).astype(BF16)
    for x in range(X):
        out_ref[:, x] = result[:, x * QUARTER : (x + 1) * QUARTER].reshape(blocks, BLOCK, QUARTER)


def experts(rows, gain, up, down):
    step = 4
    return pl.pallas_call(
        expert_kernel,
        grid=(YC // step,),
        out_shape=shape((YC, X, BLOCK, QUARTER), BF16),
        in_specs=[
            pl.BlockSpec((step, X, BLOCK, QUARTER), lambda i: (i, 0, 0, 0)),
            pl.BlockSpec((1, WIDTH), lambda i: (0, 0)),
            pl.BlockSpec((WIDTH, WIDTH), lambda i: (0, 0)),
            pl.BlockSpec((WIDTH, WIDTH), lambda i: (0, 0)),
        ],
        out_specs=pl.BlockSpec((step, X, BLOCK, QUARTER), lambda i: (i, 0, 0, 0)),
        cost_estimate=cost(4 * YC * BLOCK * WIDTH * WIDTH, 8 << 20),
        compiler_params=pltpu.CompilerParams(vmem_limit_bytes=40 << 20),
        name="experts",
    )(rows, gain, up, down)


def collect_kernel(in_ref, out_ref, wide):
    for half in range(2):
        lanes = slice(half * 128, (half + 1) * 128)
        for yc in range(YC):
            total = in_ref[yc, 0, :, lanes].astype(F32)
            for x in range(1, X):
                total = total + in_ref[yc, x, :, lanes].astype(F32)
            wide[half, pl.ds(yc, BLOCK, stride=YC)] = total
        out_ref[:, lanes] = wide[half].astype(BF16)


def combine_kernel(in_ref, pick_ref, gate_ref, mixed_ref, out_ref):
    rows = in_ref[...]
    moe = dot(pick_ref[0], rows) * gate_ref[0, :, 0:1]
    moe = moe + dot(pick_ref[1], rows) * gate_ref[1, :, 0:1]
    out_ref[...] = (mixed_ref[...] + moe).astype(BF16)


def exchange(value, axes):
    return lax.all_to_all(value, axes, split_axis=0, concat_axis=0, tiled=True)


def on_device(
    glu, dw_kernel, bn_scale, bn_shift, pw_out, block_input, ln_gain, w_up, w_down, routes, gates
):
    seq = ("z", "y", "c")
    count = Z * Y * C
    low = lax.ppermute(glu[ROWS - EDGE :], seq, [(i, i + 1) for i in range(count - 1)])
    high = lax.ppermute(glu[0:EDGE], seq, [(i + 1, i) for i in range(count - 1)])
    gain = ln_gain.reshape(1, WIDTH)
    hid_index = lax.axis_index("x").astype(jnp.int32).reshape(1)

    put, pick, gate = call(
        routing_kernel,
        (
            shape((SLOTS, ROWS), BF16),
            shape((2, ROWS, SLOTS), BF16),
            shape((2, ROWS, ROWS), F32),
        ),
        "routing",
    )(routes.T, gates.T)
    own = call(
        own_conv_kernel,
        shape((ROWS, QUARTER), F32),
        "own_conv",
        scratch=[pltpu.VMEM((ROWS + 2 * EDGE, QUARTER), F32)],
    )(glu, dw_kernel)
    parts = call(
        front_kernel,
        shape((X, ROWS + AUX, QUARTER), F32),
        "front",
        scratch=[
            pltpu.VMEM((3 * EDGE, QUARTER), F32),
            pltpu.VMEM((3 * EDGE, QUARTER), F32),
            pltpu.VMEM((ROWS, QUARTER), F32),
        ],
    )(
        own,
        low,
        high,
        dw_kernel,
        bn_scale.reshape(1, QUARTER),
        bn_shift.reshape(1, QUARTER),
        pw_out,
        block_input,
    )
    parts = exchange(parts, "x")
    mixed, rows = call(
        dispatch_kernel,
        (shape((ROWS, QUARTER), F32), shape((SLOTS, QUARTER), BF16)),
        "dispatch",
        smem=(0,),
    )(hid_index, parts, block_input, gain, put)
    rows = exchange(rows, "z")
    rows = call(
        spread_kernel,
        shape((YC, X, BLOCK, QUARTER), BF16),
        "spread",
        scratch=[pltpu.VMEM((2, SLOTS, 128), F32)],
    )(rows)
    rows = exchange(rows.reshape(YC * X, BLOCK, QUARTER), ("y", "c", "x"))
    rows = experts(rows.reshape(YC, X, BLOCK, QUARTER), gain, w_up[0], w_down[0])
    rows = exchange(rows.reshape(YC * X, BLOCK, QUARTER), ("y", "c", "x"))
    rows = call(
        collect_kernel,
        shape((SLOTS, QUARTER), BF16),
        "collect",
        scratch=[pltpu.VMEM((2, SLOTS, 128), F32)],
    )(rows.reshape(YC, X, BLOCK, QUARTER))
    rows = exchange(rows, "z")
    return call(combine_kernel, shape((ROWS, QUARTER), BF16), "combine")(rows, pick, gate, mixed)


def solution(mesh):
    chips = Mesh(mesh.devices.reshape(Z, Y, C, X), ("z", "y", "c", "x"))
    seq = ("z", "y", "c")
    in_specs = (
        P(seq, "x"),
        P(None, "x"),
        P("x"),
        P("x"),
        P("x", None),
        P(seq, None),
        P(),
        P(seq, None, "x"),
        P(seq, "x", None),
        P(seq, None),
        P(seq, None),
    )
    return jax.shard_map(
        on_device, mesh=chips, in_specs=in_specs, out_specs=P(seq, "x"), check_vma=False
    )
```

```python
import functools

import jax
import jax.numpy as jnp
from jax import lax
from jax.experimental import pallas as pl
from jax.experimental.pallas import tpu as pltpu
from jax.sharding import Mesh, PartitionSpec as P

Z, Y, C, X = 16, 4, 2, 4
YC = Y * C
ROWS = 128
QUARTER = 256
WIDTH = 1024
TAPS = 31
CAP = 6
EDGE = 16
PARTS = 1
DEPTH = CAP // PARTS
SLOTS = Z * DEPTH * YC
BLOCK = Z * DEPTH
AUX = 16

F32, BF16 = jnp.float32, jnp.bfloat16


def dot(a, b, dims=((1,), (0,))):
    return lax.dot_general(a, b, (dims, ((), ())), preferred_element_type=F32)


def silu(v):
    return v / (1.0 + jnp.exp(-v))


def cost(flops, nbytes):
    return pl.CostEstimate(flops=flops, bytes_accessed=nbytes, transcendentals=0)


def call(body, out_shape, name, flops=10**6, nbytes=10**6, scratch=(), vmem=32 << 20, smem=()):
    def whole(array):
        zeros = (0,) * len(array.shape)
        return pl.BlockSpec(array.shape, lambda i: zeros)

    def run(*args):
        in_specs = [
            pl.BlockSpec(memory_space=pltpu.SMEM) if i in smem else whole(arg)
            for i, arg in enumerate(args)
        ]
        return pl.pallas_call(
            body,
            grid=(1,),
            out_shape=out_shape,
            in_specs=in_specs,
            out_specs=jax.tree.map(whole, out_shape),
            scratch_shapes=list(scratch),
            cost_estimate=cost(flops, nbytes),
            compiler_params=pltpu.CompilerParams(vmem_limit_bytes=vmem),
            name=name,
        )(*args)

    return run


def shape(dims, dtype):
    return jax.ShapeDtypeStruct(dims, dtype)


def lanes_to_rows(row):
    return jnp.transpose(jnp.broadcast_to(row, (ROWS, ROWS)))


def routing_kernel(routes_ref, gates_ref, put_ref, pick_ref, gate_ref):
    routes = routes_ref[...]
    expert = lax.broadcasted_iota(jnp.int32, (ROWS, ROWS), 0)
    frame = lax.broadcasted_iota(jnp.int32, (ROWS, ROWS), 1)
    before = (expert < frame).astype(F32).astype(BF16)
    chosen = [(expert == routes[j : j + 1]).astype(F32) for j in range(2)]
    earlier = dot((chosen[0] + chosen[1]).astype(BF16), before)
    slot_row = lax.broadcasted_iota(jnp.int32, (SLOTS, ROWS), 0)
    slot_lane = lax.broadcasted_iota(jnp.int32, (ROWS, SLOTS), 1)
    put = [None] * PARTS
    for j in range(2):
        position = jnp.sum(chosen[j] * earlier, axis=0, keepdims=True).astype(jnp.int32)
        named = routes[j : j + 1]
        for i in range(PARTS):
            inside = (position >= i * DEPTH) & (position < (i + 1) * DEPTH)
            slot = ((named // YC) * DEPTH + position - i * DEPTH) * YC + named % YC
            slot = jnp.where(inside, slot, -1)
            here = slot_row == slot
            put[i] = here if put[i] is None else put[i] | here
            slot_col = lanes_to_rows(slot.astype(F32))[:, 0:1].astype(jnp.int32)
            pick_ref[i, j] = (slot_lane == slot_col).astype(F32).astype(BF16)
        gate_ref[j] = lanes_to_rows(gates_ref[j : j + 1])
    for i in range(PARTS):
        put_ref[i] = put[i].astype(F32).astype(BF16)


def own_conv_kernel(glu_ref, taps_ref, out_ref, padded):
    padded[0:EDGE] = jnp.zeros((EDGE, QUARTER), F32)
    padded[EDGE + ROWS :] = jnp.zeros((EDGE, QUARTER), F32)
    padded[EDGE : EDGE + ROWS] = glu_ref[...].astype(F32)
    total = None
    for k in range(TAPS):
        term = padded[k + 1 : k + 1 + ROWS] * taps_ref[k : k + 1]
        total = term if total is None else total + term
    out_ref[...] = total


def front_kernel(
    own_ref, low_ref, high_ref, taps_ref, scale_ref, shift_ref, pw_ref, input_ref, out_ref, low, high, depth
):
    low[0:EDGE] = low_ref[ROWS - EDGE :].astype(F32)
    low[EDGE:] = jnp.zeros((2 * EDGE, QUARTER), F32)
    high[0 : 2 * EDGE] = jnp.zeros((2 * EDGE, QUARTER), F32)
    high[2 * EDGE :] = high_ref[0:EDGE].astype(F32)
    depth[...] = own_ref[...]
    first, last = depth[0:EDGE], depth[ROWS - EDGE :]
    for k in range(TAPS):
        tap = taps_ref[k : k + 1]
        first = first + low[k + 1 : k + 1 + EDGE] * tap
        last = last + high[k + 1 : k + 1 + EDGE] * tap
    depth[0:EDGE] = first
    depth[ROWS - EDGE :] = last
    activated = silu(depth[...] * scale_ref[...] + shift_ref[...]).astype(BF16)
    row_sum = 0.25 * jnp.sum(input_ref[...].astype(F32), axis=1, keepdims=True)
    for x in range(X):
        part = dot(activated, pw_ref[:, x * QUARTER : (x + 1) * QUARTER])
        out_ref[x, 0:ROWS] = part.astype(BF16)
        row_sum = row_sum + jnp.sum(part, axis=1, keepdims=True)
    sums = jnp.transpose(jnp.broadcast_to(row_sum, (ROWS, ROWS)))[0:8]
    first = sums.astype(BF16).astype(F32)
    second = (sums - first).astype(BF16).astype(F32)
    third = sums - first - second
    terms = jnp.concatenate(
        [
            jnp.concatenate([first, second], axis=1),
            jnp.concatenate([third, jnp.zeros_like(third)], axis=1),
        ],
        axis=0,
    ).astype(BF16)
    for x in range(X):
        out_ref[x, ROWS:] = terms


def dispatch_kernel(x_ref, parts_ref, input_ref, gain_ref, put_ref, mixed_ref, *out_refs):
    columns = pl.ds(pl.multiple_of(x_ref[0] * QUARTER, QUARTER), QUARTER)
    mixed = input_ref[:, columns].astype(F32)
    sums = jnp.zeros((1, ROWS), F32)
    for x in range(X):
        mixed = mixed + parts_ref[x, 0:ROWS].astype(F32)
        terms = parts_ref[x, ROWS:].astype(F32)
        sums = sums + (terms[0:1, 0:ROWS] + terms[0:1, ROWS:] + terms[8:9, 0:ROWS])
    mean = lanes_to_rows(sums)[:, 0:1] * (1.0 / WIDTH)
    mixed_ref[...] = mixed
    scaled = ((mixed - mean) * gain_ref[:, columns]).astype(BF16)
    for i, out_ref in enumerate(out_refs):
        out_ref[...] = dot(put_ref[i], scaled).astype(BF16)


def spread_kernel(in_ref, out_ref, wide):
    for half in range(2):
        lanes = slice(half * 128, (half + 1) * 128)
        wide[half] = in_ref[:, lanes].astype(F32)
        for yc in range(YC):
            block = wide[half, pl.ds(yc, BLOCK, stride=YC)].astype(BF16)
            for x in range(X):
                out_ref[yc, x, :, lanes] = block


def expert_kernel(in_ref, gain_ref, up_ref, down_ref, out_ref):
    blocks = in_ref.shape[0]
    rows = jnp.concatenate(
        [in_ref[:, x].reshape(blocks * BLOCK, QUARTER) for x in range(X)], axis=1
    )
    centered = rows.astype(F32) / gain_ref[...]
    spread = jnp.sum(centered * centered, axis=1, keepdims=True) * (1.0 / WIDTH)
    inverse = 1.0 / jnp.sqrt(spread + 1e-05)
    hidden = silu(dot(rows, up_ref[...]) * inverse).astype(BF16)
    result = dot(hidden, down_ref[...]).astype(BF16)
    for x in range(X):
        out_ref[:, x] = result[:, x * QUARTER : (x + 1) * QUARTER].reshape(blocks, BLOCK, QUARTER)


def experts(rows, gain, up, down):
    step = YC if PARTS > 1 else YC // 2
    return pl.pallas_call(
        expert_kernel,
        grid=(YC // step,),
        out_shape=shape((YC, X, BLOCK, QUARTER), BF16),
        in_specs=[
            pl.BlockSpec((step, X, BLOCK, QUARTER), lambda i: (i, 0, 0, 0)),
            pl.BlockSpec((1, WIDTH), lambda i: (0, 0)),
            pl.BlockSpec((WIDTH, WIDTH), lambda i: (0, 0)),
            pl.BlockSpec((WIDTH, WIDTH), lambda i: (0, 0)),
        ],
        out_specs=pl.BlockSpec((step, X, BLOCK, QUARTER), lambda i: (i, 0, 0, 0)),
        cost_estimate=cost(4 * YC * BLOCK * WIDTH * WIDTH, 8 << 20),
        compiler_params=pltpu.CompilerParams(vmem_limit_bytes=40 << 20),
        name="experts",
    )(rows, gain, up, down)


def collect_kernel(in_ref, out_ref, wide):
    for half in range(2):
        lanes = slice(half * 128, (half + 1) * 128)
        for yc in range(YC):
            total = in_ref[yc, 0, :, lanes].astype(F32)
            for x in range(1, X):
                total = total + in_ref[yc, x, :, lanes].astype(F32)
            wide[half, pl.ds(yc, BLOCK, stride=YC)] = total
        out_ref[:, lanes] = wide[half].astype(BF16)


def combine_kernel(pick_ref, gate_ref, mixed_ref, *refs):
    out_ref = refs[PARTS]
    picked = [0.0, 0.0]
    for i in range(PARTS):
        rows = refs[i][...]
        for j in range(2):
            picked[j] = picked[j] + dot(pick_ref[i, j], rows)
    moe = picked[0] * gate_ref[0, :, 0:1] + picked[1] * gate_ref[1, :, 0:1]
    out_ref[...] = (mixed_ref[...] + moe).astype(BF16)


def exchange(value, axes):
    return lax.all_to_all(value, axes, split_axis=0, concat_axis=0, tiled=True)


def on_device(
    glu, dw_kernel, bn_scale, bn_shift, pw_out, block_input, ln_gain, w_up, w_down, routes, gates
):
    seq = ("z", "y", "c")
    count = Z * Y * C
    low = lax.ppermute(glu, seq, [(i, i + 1) for i in range(count - 1)])
    high = lax.ppermute(glu, seq, [(i + 1, i) for i in range(count - 1)])
    gain = ln_gain.reshape(1, WIDTH)
    hid_index = lax.axis_index("x").astype(jnp.int32).reshape(1)

    put, pick, gate = call(
        routing_kernel,
        (
            shape((PARTS, SLOTS, ROWS), BF16),
            shape((PARTS, 2, ROWS, SLOTS), BF16),
            shape((2, ROWS, ROWS), F32),
        ),
        "routing",
    )(routes.T, gates.T)
    own = call(
        own_conv_kernel,
        shape((ROWS, QUARTER), F32),
        "own_conv",
        vmem=60 << 20,
        scratch=[pltpu.VMEM((ROWS + 2 * EDGE, QUARTER), F32)],
    )(glu, dw_kernel)
    parts = call(
        front_kernel,
        shape((X, ROWS + AUX, QUARTER), BF16),
        "front",
        vmem=60 << 20,
        scratch=[
            pltpu.VMEM((3 * EDGE, QUARTER), F32),
            pltpu.VMEM((3 * EDGE, QUARTER), F32),
            pltpu.VMEM((ROWS, QUARTER), F32),
        ],
    )(
        own,
        low,
        high,
        dw_kernel,
        bn_scale.reshape(1, QUARTER),
        bn_shift.reshape(1, QUARTER),
        pw_out,
        block_input,
    )
    parts = exchange(parts, "x")
    mixed, *sent = call(
        dispatch_kernel,
        (shape((ROWS, QUARTER), F32),) + (shape((SLOTS, QUARTER), BF16),) * PARTS,
        "dispatch",
        smem=(0,),
    )(hid_index, parts, block_input, gain, put)
    back = []
    for rows in sent:
        rows = exchange(rows, "z")
        rows = call(
            spread_kernel,
            shape((YC, X, BLOCK, QUARTER), BF16),
            "spread",
            scratch=[pltpu.VMEM((2, SLOTS, 128), F32)],
        )(rows)
        rows = exchange(rows.reshape(YC * X, BLOCK, QUARTER), ("y", "c", "x"))
        rows = experts(rows.reshape(YC, X, BLOCK, QUARTER), gain, w_up[0], w_down[0])
        rows = exchange(rows.reshape(YC * X, BLOCK, QUARTER), ("y", "c", "x"))
        rows = call(
            collect_kernel,
            shape((SLOTS, QUARTER), BF16),
            "collect",
            scratch=[pltpu.VMEM((2, SLOTS, 128), F32)],
        )(rows.reshape(YC, X, BLOCK, QUARTER))
        back.append(exchange(rows, "z"))
    return call(combine_kernel, shape((ROWS, QUARTER), BF16), "combine")(pick, gate, mixed, *back)


def solution(mesh):
    chips = Mesh(mesh.devices.reshape(Z, Y, C, X), ("z", "y", "c", "x"))
    seq = ("z", "y", "c")
    in_specs = (
        P(seq, "x"),
        P(None, "x"),
        P("x"),
        P("x"),
        P("x", None),
        P(seq, None),
        P(),
        P(seq, None, "x"),
        P(seq, "x", None),
        P(seq, None),
        P(seq, None),
    )
    return jax.shard_map(
        on_device, mesh=chips, in_specs=in_specs, out_specs=P(seq, "x"), check_vma=False
    )
```

```python
import functools

import jax
import jax.numpy as jnp
from jax import lax
from jax.experimental import pallas as pl
from jax.experimental.pallas import tpu as pltpu
from jax.sharding import Mesh, PartitionSpec as P

Z, Y, C, X = 16, 4, 2, 4
YC = Y * C
ROWS = 128
QUARTER = 256
WIDTH = 1024
TAPS = 31
CAP = 6
EDGE = 16
SLOTS = Z * CAP * YC
BLOCK = Z * CAP
SHORT = 32
PACKED = Z * SHORT
AUX = 16

F32, BF16 = jnp.float32, jnp.bfloat16


def dot(a, b, dims=((1,), (0,))):
    return lax.dot_general(a, b, (dims, ((), ())), preferred_element_type=F32)


def silu(v):
    return v / (1.0 + jnp.exp(-v))


def cost(flops, nbytes):
    return pl.CostEstimate(flops=flops, bytes_accessed=nbytes, transcendentals=0)


def call(body, out_shape, name, flops=10**6, nbytes=10**6, scratch=(), vmem=32 << 20, smem=()):
    def whole(array):
        zeros = (0,) * len(array.shape)
        return pl.BlockSpec(array.shape, lambda i: zeros)

    def run(*args):
        in_specs = [
            pl.BlockSpec(memory_space=pltpu.SMEM) if i in smem else whole(arg)
            for i, arg in enumerate(args)
        ]
        return pl.pallas_call(
            body,
            grid=(1,),
            out_shape=out_shape,
            in_specs=in_specs,
            out_specs=jax.tree.map(whole, out_shape),
            scratch_shapes=list(scratch),
            cost_estimate=cost(flops, nbytes),
            compiler_params=pltpu.CompilerParams(vmem_limit_bytes=vmem),
            name=name,
        )(*args)

    return run


def shape(dims, dtype):
    return jax.ShapeDtypeStruct(dims, dtype)


def lanes_to_rows(row):
    return jnp.transpose(jnp.broadcast_to(row, (ROWS, ROWS)))


def ranks(routes):
    expert = lax.broadcasted_iota(jnp.int32, (ROWS, ROWS), 0)
    frame = lax.broadcasted_iota(jnp.int32, (ROWS, ROWS), 1)
    before = (expert < frame).astype(F32).astype(BF16)
    chosen = [(expert == routes[j : j + 1]).astype(F32) for j in range(2)]
    both = chosen[0] + chosen[1]
    return expert, frame, chosen, both, dot(both.astype(BF16), before)


def place(slots, count):
    row = lax.broadcasted_iota(jnp.int32, (count, ROWS), 0)
    lane = lax.broadcasted_iota(jnp.int32, (ROWS, count), 1)
    put = ((row == slots[0]) | (row == slots[1])).astype(F32).astype(BF16)
    picks = [
        (lane == lanes_to_rows(slot.astype(F32))[:, 0:1].astype(jnp.int32)).astype(F32).astype(BF16)
        for slot in slots
    ]
    return put, picks


def full_routing_kernel(routes_ref, put_ref, pick_ref):
    routes = routes_ref[...]
    _, _, chosen, _, earlier = ranks(routes)
    slots = []
    for j in range(2):
        position = jnp.sum(chosen[j] * earlier, axis=0, keepdims=True).astype(jnp.int32)
        named = routes[j : j + 1]
        slots.append(((named // YC) * CAP + position) * YC + named % YC)
    put, picks = place(slots, SLOTS)
    put_ref[...] = put
    for j in range(2):
        pick_ref[j] = picks[j]


def routing_kernel(routes_ref, gates_ref, put_ref, counts_ref, pick_ref, gate_ref):
    routes = routes_ref[...]
    expert, frame, chosen, both, earlier = ranks(routes)
    count = jnp.broadcast_to(jnp.sum(both, axis=1, keepdims=True), (ROWS, ROWS))
    lower = ((frame // YC == expert // YC) & (frame < expert)).astype(F32).astype(BF16)
    start = dot(lower, count.astype(BF16))
    too_many = jnp.max(start + count) > SHORT - 1
    slots = []
    for j in range(2):
        rank = jnp.sum(chosen[j] * (earlier + start), axis=0, keepdims=True).astype(jnp.int32)
        named = routes[j : j + 1]
        slots.append(jnp.where(rank < SHORT - 1, (named // YC) * SHORT + rank, -1))
        gate_ref[j] = lanes_to_rows(gates_ref[j : j + 1])
    put, picks = place(slots, PACKED)
    put_ref[...] = put
    for j in range(2):
        pick_ref[j] = picks[j]
    row = lax.broadcasted_iota(jnp.int32, (PACKED, ROWS), 0)
    named = lax.broadcasted_iota(jnp.int32, (PACKED, ROWS), 1)
    last = (row == (named // YC) * SHORT + SHORT - 1).astype(F32).astype(BF16)
    flag = jnp.where(too_many, 1.0, 0.0)
    values = jnp.where(frame == expert % YC, count, 0.0)
    values = values + jnp.where((frame == YC) & (expert % YC == 0), flag, 0.0)
    counts_ref[...] = dot(last, values.astype(BF16)).astype(BF16)


def own_conv_kernel(glu_ref, taps_ref, out_ref, padded):
    padded[0:EDGE] = jnp.zeros((EDGE, QUARTER), F32)
    padded[EDGE + ROWS :] = jnp.zeros((EDGE, QUARTER), F32)
    padded[EDGE : EDGE + ROWS] = glu_ref[...].astype(F32)
    total = None
    for k in range(TAPS):
        term = padded[k + 1 : k + 1 + ROWS] * taps_ref[k : k + 1]
        total = term if total is None else total + term
    out_ref[...] = total


def front_kernel(
    own_ref, low_ref, high_ref, taps_ref, scale_ref, shift_ref, pw_ref, input_ref, out_ref, low, high, depth
):
    low[0:EDGE] = low_ref[ROWS - EDGE :].astype(F32)
    low[EDGE:] = jnp.zeros((2 * EDGE, QUARTER), F32)
    high[0 : 2 * EDGE] = jnp.zeros((2 * EDGE, QUARTER), F32)
    high[2 * EDGE :] = high_ref[0:EDGE].astype(F32)
    depth[...] = own_ref[...]
    first, last = depth[0:EDGE], depth[ROWS - EDGE :]
    for k in range(TAPS):
        tap = taps_ref[k : k + 1]
        first = first + low[k + 1 : k + 1 + EDGE] * tap
        last = last + high[k + 1 : k + 1 + EDGE] * tap
    depth[0:EDGE] = first
    depth[ROWS - EDGE :] = last
    activated = silu(depth[...] * scale_ref[...] + shift_ref[...]).astype(BF16)
    row_sum = 0.25 * jnp.sum(input_ref[...].astype(F32), axis=1, keepdims=True)
    for x in range(X):
        part = dot(activated, pw_ref[:, x * QUARTER : (x + 1) * QUARTER])
        out_ref[x, 0:ROWS] = part.astype(BF16)
        row_sum = row_sum + jnp.sum(part, axis=1, keepdims=True)
    sums = jnp.transpose(jnp.broadcast_to(row_sum, (ROWS, ROWS)))[0:8]
    first = sums.astype(BF16).astype(F32)
    second = (sums - first).astype(BF16).astype(F32)
    third = sums - first - second
    terms = jnp.concatenate(
        [
            jnp.concatenate([first, second], axis=1),
            jnp.concatenate([third, jnp.zeros_like(third)], axis=1),
        ],
        axis=0,
    ).astype(BF16)
    for x in range(X):
        out_ref[x, ROWS:] = terms


def dispatch_kernel(
    x_ref, parts_ref, input_ref, gain_ref, put_ref, counts_ref, mixed_ref, scaled_ref, out_ref
):
    columns = pl.ds(pl.multiple_of(x_ref[0] * QUARTER, QUARTER), QUARTER)
    mixed = input_ref[:, columns].astype(F32)
    sums = jnp.zeros((1, ROWS), F32)
    for x in range(X):
        mixed = mixed + parts_ref[x, 0:ROWS].astype(F32)
        terms = parts_ref[x, ROWS:].astype(F32)
        sums = sums + (terms[0:1, 0:ROWS] + terms[0:1, ROWS:] + terms[8:9, 0:ROWS])
    mean = lanes_to_rows(sums)[:, 0:1] * (1.0 / WIDTH)
    mixed_ref[...] = mixed
    scaled = ((mixed - mean) * gain_ref[:, columns]).astype(BF16)
    scaled_ref[...] = scaled
    out_ref[...] = dot(put_ref[...], scaled).astype(BF16)
    for z in range(Z):
        tail = pl.ds(z * SHORT + SHORT - 16, 16)
        out_ref[tail, 0:ROWS] = out_ref[tail, 0:ROWS] + counts_ref[tail]


def full_dispatch_kernel(scaled_ref, put_ref, out_ref):
    out_ref[...] = dot(put_ref[...], scaled_ref[...]).astype(BF16)


def full_spread_kernel(in_ref, out_ref, wide):
    for half in range(2):
        lanes = slice(half * 128, (half + 1) * 128)
        wide[half] = in_ref[:, lanes].astype(F32)
        for yc in range(YC):
            block = wide[half, pl.ds(yc, BLOCK, stride=YC)].astype(BF16)
            for x in range(X):
                out_ref[yc, x, :, lanes] = block


def spread_kernel(in_ref, out_ref, source_ref, wide):
    rows = in_ref[...]
    wide[...] = rows[:, 0:ROWS].astype(F32)
    lane = lax.broadcasted_iota(jnp.int32, (Z, ROWS), 1)
    counts = wide[pl.ds(SHORT - 1, Z, stride=SHORT)]
    counts = jnp.where(lane < YC, counts, 0.0).astype(BF16)
    lower = lax.broadcasted_iota(jnp.int32, (ROWS, ROWS), 0)
    upper = lax.broadcasted_iota(jnp.int32, (ROWS, ROWS), 1)
    starts = dot(counts, (lower < upper).astype(F32).astype(BF16)).astype(BF16)
    row = lax.broadcasted_iota(jnp.int32, (BLOCK, Z), 0)
    sender = (row // CAP == lax.broadcasted_iota(jnp.int32, (BLOCK, Z), 1)).astype(F32).astype(BF16)
    row = lax.broadcasted_iota(jnp.int32, (BLOCK, ROWS), 0)
    position = (row % CAP).astype(F32)
    source = (row // CAP * SHORT).astype(F32) + dot(sender, starts) + position
    source = jnp.where(position < dot(sender, counts), source, -1.0)
    packed = lax.broadcasted_iota(jnp.int32, (BLOCK, PACKED), 1).astype(F32)
    for yc in range(YC):
        take = (packed == source[:, yc : yc + 1]).astype(F32).astype(BF16)
        block = dot(take, rows).astype(BF16)
        for x in range(X):
            out_ref[yc, x] = block
    source = jnp.concatenate([source, jnp.full((ROWS - BLOCK, ROWS), -1.0, F32)], axis=0)
    source_ref[...] = jnp.transpose(source)[0:YC]


def expert_kernel(in_ref, gain_ref, up_ref, down_ref, out_ref):
    blocks = in_ref.shape[0]
    rows = jnp.concatenate(
        [in_ref[:, x].reshape(blocks * BLOCK, QUARTER) for x in range(X)], axis=1
    )
    centered = rows.astype(F32) / gain_ref[...]
    spread = jnp.sum(centered * centered, axis=1, keepdims=True) * (1.0 / WIDTH)
    inverse = 1.0 / jnp.sqrt(spread + 1e-05)
    hidden = silu(dot(rows, up_ref[...]) * inverse).astype(BF16)
    result = dot(hidden, down_ref[...]).astype(BF16)
    for x in range(X):
        out_ref[:, x] = result[:, x * QUARTER : (x + 1) * QUARTER].reshape(blocks, BLOCK, QUARTER)


def experts(rows, gain, up, down):
    step = YC // 2
    return pl.pallas_call(
        expert_kernel,
        grid=(YC // step,),
        out_shape=shape((YC, X, BLOCK, QUARTER), BF16),
        in_specs=[
            pl.BlockSpec((step, X, BLOCK, QUARTER), lambda i: (i, 0, 0, 0)),
            pl.BlockSpec((1, WIDTH), lambda i: (0, 0)),
            pl.BlockSpec((WIDTH, WIDTH), lambda i: (0, 0)),
            pl.BlockSpec((WIDTH, WIDTH), lambda i: (0, 0)),
        ],
        out_specs=pl.BlockSpec((step, X, BLOCK, QUARTER), lambda i: (i, 0, 0, 0)),
        cost_estimate=cost(4 * YC * BLOCK * WIDTH * WIDTH, 8 << 20),
        compiler_params=pltpu.CompilerParams(vmem_limit_bytes=40 << 20),
        name="experts",
    )(rows, gain, up, down)


def summed(in_ref, yc, lanes=slice(None)):
    total = in_ref[yc, 0, :, lanes].astype(F32)
    for x in range(1, X):
        total = total + in_ref[yc, x, :, lanes].astype(F32)
    return total


def full_collect_kernel(in_ref, out_ref, wide):
    for half in range(2):
        lanes = slice(half * 128, (half + 1) * 128)
        for yc in range(YC):
            wide[half, pl.ds(yc, BLOCK, stride=YC)] = summed(in_ref, yc, lanes)
        out_ref[:, lanes] = wide[half].astype(BF16)


def collect_kernel(in_ref, source_ref, out_ref):
    packed = lax.broadcasted_iota(jnp.int32, (PACKED, BLOCK), 0).astype(F32)
    result = jnp.zeros((PACKED, QUARTER), F32)
    for yc in range(YC):
        give = (packed == source_ref[yc : yc + 1, 0:BLOCK]).astype(F32).astype(BF16)
        result = result + dot(give, summed(in_ref, yc).astype(BF16))
    out_ref[...] = result.astype(BF16)


def combine_kernel(in_ref, pick_ref, gate_ref, mixed_ref, out_ref):
    rows = in_ref[...]
    moe = dot(pick_ref[0], rows) * gate_ref[0, :, 0:1]
    moe = moe + dot(pick_ref[1], rows) * gate_ref[1, :, 0:1]
    out_ref[...] = (mixed_ref[...] + moe).astype(BF16)


def exchange(value, axes):
    return lax.all_to_all(value, axes, split_axis=0, concat_axis=0, tiled=True)


def on_device(
    glu, dw_kernel, bn_scale, bn_shift, pw_out, block_input, ln_gain, w_up, w_down, routes, gates
):
    seq = ("z", "y", "c")
    count = Z * Y * C
    low = lax.ppermute(glu, seq, [(i, i + 1) for i in range(count - 1)])
    high = lax.ppermute(glu, seq, [(i + 1, i) for i in range(count - 1)])
    gain = ln_gain.reshape(1, WIDTH)
    hid_index = lax.axis_index("x").astype(jnp.int32).reshape(1)

    put, counts, pick, gate = call(
        routing_kernel,
        (
            shape((PACKED, ROWS), BF16),
            shape((PACKED, ROWS), BF16),
            shape((2, ROWS, PACKED), BF16),
            shape((2, ROWS, ROWS), F32),
        ),
        "routing",
    )(routes.T, gates.T)
    own = call(
        own_conv_kernel,
        shape((ROWS, QUARTER), F32),
        "own_conv",
        vmem=60 << 20,
        scratch=[pltpu.VMEM((ROWS + 2 * EDGE, QUARTER), F32)],
    )(glu, dw_kernel)
    parts = call(
        front_kernel,
        shape((X, ROWS + AUX, QUARTER), BF16),
        "front",
        vmem=60 << 20,
        scratch=[
            pltpu.VMEM((3 * EDGE, QUARTER), F32),
            pltpu.VMEM((3 * EDGE, QUARTER), F32),
            pltpu.VMEM((ROWS, QUARTER), F32),
        ],
    )(
        own,
        low,
        high,
        dw_kernel,
        bn_scale.reshape(1, QUARTER),
        bn_shift.reshape(1, QUARTER),
        pw_out,
        block_input,
    )
    parts = exchange(parts, "x")
    mixed, scaled, rows = call(
        dispatch_kernel,
        (
            shape((ROWS, QUARTER), F32),
            shape((ROWS, QUARTER), BF16),
            shape((PACKED, QUARTER), BF16),
        ),
        "dispatch",
        smem=(0,),
    )(hid_index, parts, block_input, gain, put, counts)
    rows = exchange(rows, "z")
    flags = rows.reshape(Z, SHORT, QUARTER)[:, SHORT - 1, YC]
    crowded = jnp.max(flags.astype(F32)) > 0.5

    def full_slots():
        return call(
            full_routing_kernel,
            (shape((SLOTS, ROWS), BF16), shape((2, ROWS, SLOTS), BF16)),
            "full_routing",
        )(routes.T)

    def full_out(_):
        sent = call(full_dispatch_kernel, shape((SLOTS, QUARTER), BF16), "full_dispatch")(
            scaled, full_slots()[0]
        )
        blocks = call(
            full_spread_kernel,
            shape((YC, X, BLOCK, QUARTER), BF16),
            "full_spread",
            scratch=[pltpu.VMEM((2, SLOTS, 128), F32)],
        )(exchange(sent, "z"))
        return blocks, jnp.zeros((YC, ROWS), F32)

    def short_out(packed):
        return call(
            spread_kernel,
            (shape((YC, X, BLOCK, QUARTER), BF16), shape((YC, ROWS), F32)),
            "spread",
            scratch=[pltpu.VMEM((PACKED, ROWS), F32)],
        )(packed)

    rows, source = lax.cond(crowded, full_out, short_out, rows)
    rows = exchange(rows.reshape(YC * X, BLOCK, QUARTER), ("y", "c", "x"))
    rows = experts(rows.reshape(YC, X, BLOCK, QUARTER), gain, w_up[0], w_down[0])
    rows = exchange(rows.reshape(YC * X, BLOCK, QUARTER), ("y", "c", "x"))
    rows = rows.reshape(YC, X, BLOCK, QUARTER)

    def full_back(blocks):
        sent = call(
            full_collect_kernel,
            shape((SLOTS, QUARTER), BF16),
            "full_collect",
            scratch=[pltpu.VMEM((2, SLOTS, 128), F32)],
        )(blocks)
        return call(combine_kernel, shape((ROWS, QUARTER), BF16), "full_combine")(
            exchange(sent, "z"), full_slots()[1], gate, mixed
        )

    def short_back(blocks):
        sent = call(collect_kernel, shape((PACKED, QUARTER), BF16), "collect")(blocks, source)
        return call(combine_kernel, shape((ROWS, QUARTER), BF16), "combine")(
            exchange(sent, "z"), pick, gate, mixed
        )

    return lax.cond(crowded, full_back, short_back, rows)


def solution(mesh):
    chips = Mesh(mesh.devices.reshape(Z, Y, C, X), ("z", "y", "c", "x"))
    seq = ("z", "y", "c")
    in_specs = (
        P(seq, "x"),
        P(None, "x"),
        P("x"),
        P("x"),
        P("x", None),
        P(seq, None),
        P(),
        P(seq, None, "x"),
        P(seq, "x", None),
        P(seq, None),
        P(seq, None),
    )
    return jax.shard_map(
        on_device, mesh=chips, in_specs=in_specs, out_specs=P(seq, "x"), check_vma=False
    )
```

```python
import functools

import jax
import jax.numpy as jnp
from jax import lax
from jax.experimental import pallas as pl
from jax.experimental.pallas import tpu as pltpu
from jax.sharding import Mesh, PartitionSpec as P

Z, Y, C, X = 16, 4, 2, 4
YC = Y * C
ROWS = 128
QUARTER = 256
WIDTH = 1024
TAPS = 31
CAP = 6
EDGE = 16
SLOTS = Z * CAP * YC
BLOCK = Z * CAP
SHORT = 32
PACKED = Z * SHORT
AUX = 16

F32, BF16 = jnp.float32, jnp.bfloat16


def dot(a, b, dims=((1,), (0,))):
    return lax.dot_general(a, b, (dims, ((), ())), preferred_element_type=F32)


def silu(v):
    return v / (1.0 + jnp.exp(-v))


def cost(flops, nbytes):
    return pl.CostEstimate(flops=flops, bytes_accessed=nbytes, transcendentals=0)


def call(body, out_shape, name, flops=10**6, nbytes=10**6, scratch=(), vmem=32 << 20, smem=()):
    def whole(array):
        zeros = (0,) * len(array.shape)
        return pl.BlockSpec(array.shape, lambda i: zeros)

    def run(*args):
        in_specs = [
            pl.BlockSpec(memory_space=pltpu.SMEM) if i in smem else whole(arg)
            for i, arg in enumerate(args)
        ]
        return pl.pallas_call(
            body,
            grid=(1,),
            out_shape=out_shape,
            in_specs=in_specs,
            out_specs=jax.tree.map(whole, out_shape),
            scratch_shapes=list(scratch),
            cost_estimate=cost(flops, nbytes),
            compiler_params=pltpu.CompilerParams(vmem_limit_bytes=vmem),
            name=name,
        )(*args)

    return run


def shape(dims, dtype):
    return jax.ShapeDtypeStruct(dims, dtype)


def lanes_to_rows(row):
    return jnp.transpose(jnp.broadcast_to(row, (ROWS, ROWS)))


def ranks(routes):
    expert = lax.broadcasted_iota(jnp.int32, (ROWS, ROWS), 0)
    frame = lax.broadcasted_iota(jnp.int32, (ROWS, ROWS), 1)
    before = (expert < frame).astype(F32).astype(BF16)
    chosen = [(expert == routes[j : j + 1]).astype(F32) for j in range(2)]
    both = chosen[0] + chosen[1]
    return expert, frame, chosen, both, dot(both.astype(BF16), before)


def place(slots, count):
    row = lax.broadcasted_iota(jnp.int32, (count, ROWS), 0)
    lane = lax.broadcasted_iota(jnp.int32, (ROWS, count), 1)
    put = ((row == slots[0]) | (row == slots[1])).astype(F32).astype(BF16)
    picks = [
        (lane == lanes_to_rows(slot.astype(F32))[:, 0:1].astype(jnp.int32)).astype(F32).astype(BF16)
        for slot in slots
    ]
    return put, picks


def full_routing_kernel(routes_ref, put_ref, pick_ref):
    routes = routes_ref[...]
    _, _, chosen, _, earlier = ranks(routes)
    slots = []
    for j in range(2):
        position = jnp.sum(chosen[j] * earlier, axis=0, keepdims=True).astype(jnp.int32)
        named = routes[j : j + 1]
        slots.append(((named // YC) * CAP + position) * YC + named % YC)
    put, picks = place(slots, SLOTS)
    put_ref[...] = put
    for j in range(2):
        pick_ref[j] = picks[j]


def routing_kernel(routes_ref, gates_ref, put_ref, counts_ref, pick_ref, gate_ref):
    routes = routes_ref[...]
    expert, frame, chosen, both, earlier = ranks(routes)
    count = jnp.broadcast_to(jnp.sum(both, axis=1, keepdims=True), (ROWS, ROWS))
    lower = ((frame // YC == expert // YC) & (frame < expert)).astype(F32).astype(BF16)
    start = dot(lower, count.astype(BF16))
    too_many = jnp.max(start + count) > SHORT - 1
    slots = []
    for j in range(2):
        rank = jnp.sum(chosen[j] * (earlier + start), axis=0, keepdims=True).astype(jnp.int32)
        named = routes[j : j + 1]
        slots.append(jnp.where(rank < SHORT - 1, (named // YC) * SHORT + rank, -1))
        gate_ref[j] = lanes_to_rows(gates_ref[j : j + 1])
    put, picks = place(slots, PACKED)
    put_ref[...] = put
    for j in range(2):
        pick_ref[j] = picks[j]
    row = lax.broadcasted_iota(jnp.int32, (PACKED, ROWS), 0)
    named = lax.broadcasted_iota(jnp.int32, (PACKED, ROWS), 1)
    last = (row == (named // YC) * SHORT + SHORT - 1).astype(F32).astype(BF16)
    flag = jnp.where(too_many, 1.0, 0.0)
    values = jnp.where(frame == expert % YC, count, 0.0)
    values = values + jnp.where((frame == YC) & (expert % YC == 0), flag, 0.0)
    counts_ref[...] = dot(last, values.astype(BF16)).astype(BF16)


def own_conv_kernel(glu_ref, taps_ref, out_ref, same_ref, padded):
    padded[0:EDGE] = jnp.zeros((EDGE, QUARTER), F32)
    padded[EDGE + ROWS :] = jnp.zeros((EDGE, QUARTER), F32)
    padded[EDGE : EDGE + ROWS] = glu_ref[...].astype(F32)
    total = None
    for k in range(TAPS):
        term = padded[k + 1 : k + 1 + ROWS] * taps_ref[k : k + 1]
        total = term if total is None else total + term
    out_ref[...] = total
    same_ref[...] = glu_ref[...]


def front_kernel(
    core_ref, own_ref, beyond_ref, beside_ref, taps_ref, scale_ref, shift_ref, pw_ref, input_ref, out_ref, low, high, depth
):
    first_core = core_ref[0] == 0
    tail = pl.ds(ROWS - EDGE, EDGE)
    head = pl.ds(0, EDGE)
    low[0:EDGE] = jnp.where(first_core, beyond_ref[tail].astype(F32), beside_ref[tail].astype(F32))
    low[EDGE:] = jnp.zeros((2 * EDGE, QUARTER), F32)
    high[0 : 2 * EDGE] = jnp.zeros((2 * EDGE, QUARTER), F32)
    high[2 * EDGE :] = jnp.where(
        first_core, beside_ref[head].astype(F32), beyond_ref[head].astype(F32)
    )
    depth[...] = own_ref[...]
    first, last = depth[0:EDGE], depth[ROWS - EDGE :]
    for k in range(TAPS):
        tap = taps_ref[k : k + 1]
        first = first + low[k + 1 : k + 1 + EDGE] * tap
        last = last + high[k + 1 : k + 1 + EDGE] * tap
    depth[0:EDGE] = first
    depth[ROWS - EDGE :] = last
    activated = silu(depth[...] * scale_ref[...] + shift_ref[...]).astype(BF16)
    row_sum = 0.25 * jnp.sum(input_ref[...].astype(F32), axis=1, keepdims=True)
    for x in range(X):
        part = dot(activated, pw_ref[:, x * QUARTER : (x + 1) * QUARTER])
        out_ref[x, 0:ROWS] = part.astype(BF16)
        row_sum = row_sum + jnp.sum(part, axis=1, keepdims=True)
    sums = jnp.transpose(jnp.broadcast_to(row_sum, (ROWS, ROWS)))[0:8]
    first = sums.astype(BF16).astype(F32)
    second = (sums - first).astype(BF16).astype(F32)
    third = sums - first - second
    terms = jnp.concatenate(
        [
            jnp.concatenate([first, second], axis=1),
            jnp.concatenate([third, jnp.zeros_like(third)], axis=1),
        ],
        axis=0,
    ).astype(BF16)
    for x in range(X):
        out_ref[x, ROWS:] = terms


def dispatch_kernel(
    x_ref, parts_ref, input_ref, gain_ref, put_ref, counts_ref, mixed_ref, scaled_ref, out_ref
):
    columns = pl.ds(pl.multiple_of(x_ref[0] * QUARTER, QUARTER), QUARTER)
    mixed = input_ref[:, columns].astype(F32)
    sums = jnp.zeros((1, ROWS), F32)
    for x in range(X):
        mixed = mixed + parts_ref[x, 0:ROWS].astype(F32)
        terms = parts_ref[x, ROWS:].astype(F32)
        sums = sums + (terms[0:1, 0:ROWS] + terms[0:1, ROWS:] + terms[8:9, 0:ROWS])
    mean = lanes_to_rows(sums)[:, 0:1] * (1.0 / WIDTH)
    mixed_ref[...] = mixed
    scaled = ((mixed - mean) * gain_ref[:, columns]).astype(BF16)
    scaled_ref[...] = scaled
    sent = dot(put_ref[...], scaled)
    out_ref[:, 0:ROWS] = (sent[:, 0:ROWS] + counts_ref[...].astype(F32)).astype(BF16)
    out_ref[:, ROWS:] = sent[:, ROWS:].astype(BF16)


def full_dispatch_kernel(scaled_ref, put_ref, out_ref):
    out_ref[...] = dot(put_ref[...], scaled_ref[...]).astype(BF16)


def full_spread_kernel(in_ref, out_ref, wide):
    for half in range(2):
        lanes = slice(half * 128, (half + 1) * 128)
        wide[half] = in_ref[:, lanes].astype(F32)
        for yc in range(YC):
            block = wide[half, pl.ds(yc, BLOCK, stride=YC)].astype(BF16)
            for x in range(X):
                out_ref[yc, x, :, lanes] = block


def spread_kernel(in_ref, out_ref, source_ref, wide):
    rows = in_ref[...]
    wide[...] = rows[:, 0:ROWS].astype(F32)
    lane = lax.broadcasted_iota(jnp.int32, (Z, ROWS), 1)
    counts = wide[pl.ds(SHORT - 1, Z, stride=SHORT)]
    crowded = jnp.max(jnp.where(lane == YC, counts, 0.0), axis=(0, 1), keepdims=True) > 0.5
    mark = jnp.where(crowded, jnp.inf, 0.0)
    counts = jnp.where(lane < YC, counts, 0.0).astype(BF16)
    lower = lax.broadcasted_iota(jnp.int32, (ROWS, ROWS), 0)
    upper = lax.broadcasted_iota(jnp.int32, (ROWS, ROWS), 1)
    starts = dot(counts, (lower < upper).astype(F32).astype(BF16)).astype(BF16)
    row = lax.broadcasted_iota(jnp.int32, (BLOCK, Z), 0)
    sender = (row // CAP == lax.broadcasted_iota(jnp.int32, (BLOCK, Z), 1)).astype(F32).astype(BF16)
    row = lax.broadcasted_iota(jnp.int32, (BLOCK, ROWS), 0)
    position = (row % CAP).astype(F32)
    source = (row // CAP * SHORT).astype(F32) + dot(sender, starts) + position
    source = jnp.where(position < dot(sender, counts), source, -1.0)
    rows_half, block_half = PACKED // 2, BLOCK // 2
    packed = lax.broadcasted_iota(jnp.int32, (block_half, rows_half), 1).astype(F32)
    for half in range(2):
        mine = pl.ds(half * block_half, block_half)
        wanted = source[half * block_half : (half + 1) * block_half] - float(half * rows_half)
        take = jnp.concatenate(
            [(packed == wanted[:, yc : yc + 1]).astype(F32).astype(BF16) for yc in range(YC)],
            axis=0,
        )
        blocks = dot(take, rows[half * rows_half : (half + 1) * rows_half])
        blocks = (blocks + mark).astype(BF16)
        for yc in range(YC):
            for x in range(X):
                out_ref[yc, x, mine] = blocks[yc * block_half : (yc + 1) * block_half]
    source = jnp.concatenate([source, jnp.full((ROWS - BLOCK, ROWS), -1.0, F32)], axis=0)
    source_ref[...] = jnp.transpose(source)[0:YC]


def expert_kernel(in_ref, gain_ref, up_ref, down_ref, out_ref, mark_ref):
    blocks = in_ref.shape[0]
    rows = jnp.concatenate(
        [in_ref[:, x].reshape(blocks * BLOCK, QUARTER) for x in range(X)], axis=1
    )
    centered = rows.astype(F32) * (1.0 / gain_ref[...])
    spread = jnp.sum(centered * centered, axis=1, keepdims=True) * (1.0 / WIDTH)
    marked = jnp.where(jnp.max(spread) == jnp.inf, 1, 0)

    @pl.when(pl.program_id(0) == 0)
    def _():
        mark_ref[0] = marked

    @pl.when(pl.program_id(0) > 0)
    def _():
        mark_ref[0] = jnp.maximum(mark_ref[0], marked)

    inverse = 1.0 / jnp.sqrt(spread + 1e-05)
    hidden = silu(dot(rows, up_ref[...]) * inverse).astype(BF16)
    result = dot(hidden, down_ref[...]).astype(BF16)
    for x in range(X):
        out_ref[:, x] = result[:, x * QUARTER : (x + 1) * QUARTER].reshape(blocks, BLOCK, QUARTER)


def experts(rows, gain, up, down):
    step = YC // 2
    return pl.pallas_call(
        expert_kernel,
        grid=(YC // step,),
        out_shape=(shape((YC, X, BLOCK, QUARTER), BF16), shape((1,), jnp.int32)),
        in_specs=[
            pl.BlockSpec((step, X, BLOCK, QUARTER), lambda i: (i, 0, 0, 0)),
            pl.BlockSpec((1, WIDTH), lambda i: (0, 0)),
            pl.BlockSpec((WIDTH, WIDTH), lambda i: (0, 0)),
            pl.BlockSpec((WIDTH, WIDTH), lambda i: (0, 0)),
        ],
        out_specs=(
            pl.BlockSpec((step, X, BLOCK, QUARTER), lambda i: (i, 0, 0, 0)),
            pl.BlockSpec(memory_space=pltpu.SMEM),
        ),
        cost_estimate=cost(4 * YC * BLOCK * WIDTH * WIDTH, 8 << 20),
        compiler_params=pltpu.CompilerParams(vmem_limit_bytes=40 << 20),
        name="experts",
    )(rows, gain, up, down)


def summed(in_ref, yc, lanes=slice(None)):
    total = in_ref[yc, 0, :, lanes].astype(F32)
    for x in range(1, X):
        total = total + in_ref[yc, x, :, lanes].astype(F32)
    return total


def full_collect_kernel(in_ref, out_ref, wide):
    for half in range(2):
        lanes = slice(half * 128, (half + 1) * 128)
        for yc in range(YC):
            wide[half, pl.ds(yc, BLOCK, stride=YC)] = summed(in_ref, yc, lanes)
        out_ref[:, lanes] = wide[half].astype(BF16)


def collect_kernel(in_ref, source_ref, out_ref):
    packed = lax.broadcasted_iota(jnp.int32, (PACKED, BLOCK), 0).astype(F32)
    result = jnp.zeros((PACKED, QUARTER), F32)
    for yc in range(YC):
        give = (packed == source_ref[yc : yc + 1, 0:BLOCK]).astype(F32).astype(BF16)
        result = result + dot(give, summed(in_ref, yc).astype(BF16))
    out_ref[...] = result.astype(BF16)


def combine_kernel(in_ref, pick_ref, gate_ref, mixed_ref, out_ref):
    rows = in_ref[...]
    moe = dot(pick_ref[0], rows) * gate_ref[0, :, 0:1]
    moe = moe + dot(pick_ref[1], rows) * gate_ref[1, :, 0:1]
    out_ref[...] = (mixed_ref[...] + moe).astype(BF16)


def exchange(value, axes):
    return lax.all_to_all(value, axes, split_axis=0, concat_axis=0, tiled=True)


def through_experts(rows, gain, w_up, w_down):
    rows = exchange(rows.reshape(YC * X, BLOCK, QUARTER), ("y", "c", "x"))
    rows, marked = experts(rows.reshape(YC, X, BLOCK, QUARTER), gain, w_up[0], w_down[0])
    rows = exchange(rows.reshape(YC * X, BLOCK, QUARTER), ("y", "c", "x"))
    return rows.reshape(YC, X, BLOCK, QUARTER), marked


def on_device(
    glu, dw_kernel, bn_scale, bn_shift, pw_out, block_input, ln_gain, w_up, w_down, routes, gates
):
    seq = ("z", "y", "c")
    count = Z * Y * C
    pairs = [(i, i + 1) for i in range(1, count - 1, 2)]
    beyond = lax.ppermute(glu, seq, pairs + [(j, i) for i, j in pairs])
    own, same = call(
        own_conv_kernel,
        (shape((ROWS, QUARTER), F32), shape((ROWS, QUARTER), BF16)),
        "own_conv",
        vmem=60 << 20,
        scratch=[pltpu.VMEM((ROWS + 2 * EDGE, QUARTER), F32)],
    )(glu, dw_kernel)
    pairs = [(i, i + 1) for i in range(0, count, 2)]
    beside = lax.ppermute(same, seq, pairs + [(j, i) for i, j in pairs])
    core = lax.axis_index("c").astype(jnp.int32).reshape(1)
    gain = ln_gain.reshape(1, WIDTH)
    hid_index = lax.axis_index("x").astype(jnp.int32).reshape(1)

    put, counts, pick, gate = call(
        routing_kernel,
        (
            shape((PACKED, ROWS), BF16),
            shape((PACKED, ROWS), BF16),
            shape((2, ROWS, PACKED), BF16),
            shape((2, ROWS, ROWS), F32),
        ),
        "routing",
    )(routes.T, gates.T)
    parts = call(
        front_kernel,
        shape((X, ROWS + AUX, QUARTER), BF16),
        "front",
        vmem=60 << 20,
        smem=(0,),
        scratch=[
            pltpu.VMEM((3 * EDGE, QUARTER), F32),
            pltpu.VMEM((3 * EDGE, QUARTER), F32),
            pltpu.VMEM((ROWS, QUARTER), F32),
        ],
    )(
        core,
        own,
        beyond,
        beside,
        dw_kernel,
        bn_scale.reshape(1, QUARTER),
        bn_shift.reshape(1, QUARTER),
        pw_out,
        block_input,
    )
    parts = exchange(parts, "x")
    mixed, scaled, rows = call(
        dispatch_kernel,
        (
            shape((ROWS, QUARTER), F32),
            shape((ROWS, QUARTER), BF16),
            shape((PACKED, QUARTER), BF16),
        ),
        "dispatch",
        smem=(0,),
    )(hid_index, parts, block_input, gain, put, counts)
    rows = exchange(rows, "z")
    rows, source = call(
        spread_kernel,
        (shape((YC, X, BLOCK, QUARTER), BF16), shape((YC, ROWS), F32)),
        "spread",
        scratch=[pltpu.VMEM((PACKED, ROWS), F32)],
    )(rows)
    rows, marked = through_experts(rows, gain, w_up, w_down)
    rows = call(collect_kernel, shape((PACKED, QUARTER), BF16), "collect")(rows, source)
    rows = exchange(rows, "z")

    def short(rows):
        return call(combine_kernel, shape((ROWS, QUARTER), BF16), "combine")(
            rows, pick, gate, mixed
        )

    def full(_):
        put, pick = call(
            full_routing_kernel,
            (shape((SLOTS, ROWS), BF16), shape((2, ROWS, SLOTS), BF16)),
            "full_routing",
        )(routes.T)
        rows = call(full_dispatch_kernel, shape((SLOTS, QUARTER), BF16), "full_dispatch")(scaled, put)
        rows = call(
            full_spread_kernel,
            shape((YC, X, BLOCK, QUARTER), BF16),
            "full_spread",
            scratch=[pltpu.VMEM((2, SLOTS, 128), F32)],
        )(exchange(rows, "z"))
        rows, _ = through_experts(rows, gain, w_up, w_down)
        rows = call(
            full_collect_kernel,
            shape((SLOTS, QUARTER), BF16),
            "full_collect",
            scratch=[pltpu.VMEM((2, SLOTS, 128), F32)],
        )(rows)
        return call(combine_kernel, shape((ROWS, QUARTER), BF16), "full_combine")(
            exchange(rows, "z"), pick, gate, mixed
        )

    return lax.cond(marked[0] > 0, full, short, rows)


def solution(mesh):
    chips = Mesh(mesh.devices.reshape(Z, Y, C, X), ("z", "y", "c", "x"))
    seq = ("z", "y", "c")
    in_specs = (
        P(seq, "x"),
        P(None, "x"),
        P("x"),
        P("x"),
        P("x", None),
        P(seq, None),
        P(),
        P(seq, None, "x"),
        P(seq, "x", None),
        P(seq, None),
        P(seq, None),
    )
    return jax.shard_map(
        on_device, mesh=chips, in_specs=in_specs, out_specs=P(seq, "x"), check_vma=False
    )
```

```python
import functools

import jax
import jax.numpy as jnp
from jax import lax
from jax.experimental import pallas as pl
from jax.experimental.pallas import tpu as pltpu
from jax.sharding import Mesh, PartitionSpec as P

Z, Y, C, X = 16, 4, 2, 4
YC = Y * C
ROWS = 128
QUARTER = 256
WIDTH = 1024
TAPS = 31
CAP = 6
EDGE = 16
SLOTS = Z * CAP * YC
BLOCK = Z * CAP
SHORT = 32
PACKED = Z * SHORT
AUX = 16

F32, BF16 = jnp.float32, jnp.bfloat16


def dot(a, b, dims=((1,), (0,))):
    return lax.dot_general(a, b, (dims, ((), ())), preferred_element_type=F32)


def silu(v):
    return v / (1.0 + jnp.exp(-v))


def cost(flops, nbytes):
    return pl.CostEstimate(flops=flops, bytes_accessed=nbytes, transcendentals=0)


def call(body, out_shape, name, flops=10**6, nbytes=10**6, scratch=(), vmem=32 << 20, smem=()):
    def whole(array):
        zeros = (0,) * len(array.shape)
        return pl.BlockSpec(array.shape, lambda i: zeros)

    def run(*args):
        in_specs = [
            pl.BlockSpec(memory_space=pltpu.SMEM) if i in smem else whole(arg)
            for i, arg in enumerate(args)
        ]
        return pl.pallas_call(
            body,
            grid=(1,),
            out_shape=out_shape,
            in_specs=in_specs,
            out_specs=jax.tree.map(whole, out_shape),
            scratch_shapes=list(scratch),
            cost_estimate=cost(flops, nbytes),
            compiler_params=pltpu.CompilerParams(vmem_limit_bytes=vmem),
            name=name,
        )(*args)

    return run


def shape(dims, dtype):
    return jax.ShapeDtypeStruct(dims, dtype)


def lanes_to_rows(row):
    return jnp.transpose(jnp.broadcast_to(row, (ROWS, ROWS)))


def ranks(routes):
    expert = lax.broadcasted_iota(jnp.int32, (ROWS, ROWS), 0)
    frame = lax.broadcasted_iota(jnp.int32, (ROWS, ROWS), 1)
    before = (expert < frame).astype(F32).astype(BF16)
    chosen = [(expert == routes[j : j + 1]).astype(F32) for j in range(2)]
    both = chosen[0] + chosen[1]
    return expert, frame, chosen, both, dot(both.astype(BF16), before)


def place(slots, count):
    row = lax.broadcasted_iota(jnp.int32, (count, ROWS), 0)
    lane = lax.broadcasted_iota(jnp.int32, (ROWS, count), 1)
    put = ((row == slots[0]) | (row == slots[1])).astype(F32).astype(BF16)
    picks = [
        (lane == lanes_to_rows(slot.astype(F32))[:, 0:1].astype(jnp.int32)).astype(F32).astype(BF16)
        for slot in slots
    ]
    return put, picks


def full_routing_kernel(routes_ref, put_ref, pick_ref):
    routes = routes_ref[...]
    _, _, chosen, _, earlier = ranks(routes)
    slots = []
    for j in range(2):
        position = jnp.sum(chosen[j] * earlier, axis=0, keepdims=True).astype(jnp.int32)
        named = routes[j : j + 1]
        slots.append(((named // YC) * CAP + position) * YC + named % YC)
    put, picks = place(slots, SLOTS)
    put_ref[...] = put
    for j in range(2):
        pick_ref[j] = picks[j]


def routing_kernel(routes_ref, gates_ref, put_ref, counts_ref, pick_ref, gate_ref):
    routes = routes_ref[...]
    expert, frame, chosen, both, earlier = ranks(routes)
    count = jnp.broadcast_to(jnp.sum(both, axis=1, keepdims=True), (ROWS, ROWS))
    lower = ((frame // YC == expert // YC) & (frame < expert)).astype(F32).astype(BF16)
    start = dot(lower, count.astype(BF16))
    too_many = jnp.max(start + count) > SHORT - 1
    slots = []
    for j in range(2):
        rank = jnp.sum(chosen[j] * (earlier + start), axis=0, keepdims=True).astype(jnp.int32)
        named = routes[j : j + 1]
        slots.append(jnp.where(rank < SHORT - 1, (named // YC) * SHORT + rank, -1))
        gate_ref[j] = lanes_to_rows(gates_ref[j : j + 1])
    put, picks = place(slots, PACKED)
    put_ref[...] = put
    for j in range(2):
        pick_ref[j] = picks[j]
    row = lax.broadcasted_iota(jnp.int32, (PACKED, ROWS), 0)
    named = lax.broadcasted_iota(jnp.int32, (PACKED, ROWS), 1)
    last = (row == (named // YC) * SHORT + SHORT - 1).astype(F32).astype(BF16)
    flag = jnp.where(too_many, 1.0, 0.0)
    values = jnp.where(frame == expert % YC, count, 0.0)
    values = values + jnp.where((frame == YC) & (expert % YC == 0), flag, 0.0)
    counts_ref[...] = dot(last, values.astype(BF16)).astype(BF16)


def edge_kernel(core_ref, glu_ref, out_ref):
    first_core = core_ref[0] == 0
    tail = glu_ref[ROWS - EDGE :].astype(F32)
    head = glu_ref[0:EDGE].astype(F32)
    out_ref[...] = jnp.where(first_core, tail, head).astype(BF16)


def own_conv_kernel(glu_ref, taps_ref, out_ref, padded):
    padded[0:EDGE] = jnp.zeros((EDGE, QUARTER), F32)
    padded[EDGE + ROWS :] = jnp.zeros((EDGE, QUARTER), F32)
    padded[EDGE : EDGE + ROWS] = glu_ref[...].astype(F32)
    total = None
    for k in range(TAPS):
        term = padded[k + 1 : k + 1 + ROWS] * taps_ref[k : k + 1]
        total = term if total is None else total + term
    out_ref[...] = total


def front_kernel(
    core_ref, own_ref, beyond_ref, beside_ref, taps_ref, scale_ref, shift_ref, pw_ref, input_ref, out_ref, low, high, depth
):
    first_core = core_ref[0] == 0
    tail = pl.ds(ROWS - EDGE, EDGE)
    head = pl.ds(0, EDGE)
    low[0:EDGE] = jnp.where(first_core, beyond_ref[tail].astype(F32), beside_ref[...].astype(F32))
    low[EDGE:] = jnp.zeros((2 * EDGE, QUARTER), F32)
    high[0 : 2 * EDGE] = jnp.zeros((2 * EDGE, QUARTER), F32)
    high[2 * EDGE :] = jnp.where(
        first_core, beside_ref[...].astype(F32), beyond_ref[head].astype(F32)
    )
    depth[...] = own_ref[...]
    first, last = depth[0:EDGE], depth[ROWS - EDGE :]
    for k in range(TAPS):
        tap = taps_ref[k : k + 1]
        first = first + low[k + 1 : k + 1 + EDGE] * tap
        last = last + high[k + 1 : k + 1 + EDGE] * tap
    depth[0:EDGE] = first
    depth[ROWS - EDGE :] = last
    activated = silu(depth[...] * scale_ref[...] + shift_ref[...]).astype(BF16)
    row_sum = 0.25 * jnp.sum(input_ref[...].astype(F32), axis=1, keepdims=True)
    for x in range(X):
        part = dot(activated, pw_ref[:, x * QUARTER : (x + 1) * QUARTER])
        out_ref[x, 0:ROWS] = part.astype(BF16)
        row_sum = row_sum + jnp.sum(part, axis=1, keepdims=True)
    sums = jnp.transpose(jnp.broadcast_to(row_sum, (ROWS, ROWS)))[0:8]
    first = sums.astype(BF16).astype(F32)
    second = (sums - first).astype(BF16).astype(F32)
    third = sums - first - second
    terms = jnp.concatenate(
        [
            jnp.concatenate([first, second], axis=1),
            jnp.concatenate([third, jnp.zeros_like(third)], axis=1),
        ],
        axis=0,
    ).astype(BF16)
    for x in range(X):
        out_ref[x, ROWS:] = terms


def dispatch_kernel(
    x_ref, parts_ref, input_ref, gain_ref, put_ref, counts_ref, mixed_ref, scaled_ref, out_ref
):
    columns = pl.ds(pl.multiple_of(x_ref[0] * QUARTER, QUARTER), QUARTER)
    mixed = input_ref[:, columns].astype(F32)
    sums = jnp.zeros((1, ROWS), F32)
    for x in range(X):
        mixed = mixed + parts_ref[x, 0:ROWS].astype(F32)
        terms = parts_ref[x, ROWS:].astype(F32)
        sums = sums + (terms[0:1, 0:ROWS] + terms[0:1, ROWS:] + terms[8:9, 0:ROWS])
    mean = lanes_to_rows(sums)[:, 0:1] * (1.0 / WIDTH)
    mixed_ref[...] = mixed
    scaled = ((mixed - mean) * gain_ref[:, columns]).astype(BF16)
    scaled_ref[...] = scaled
    sent = dot(put_ref[...], scaled)
    out_ref[:, 0:ROWS] = (sent[:, 0:ROWS] + counts_ref[...].astype(F32)).astype(BF16)
    out_ref[:, ROWS:] = sent[:, ROWS:].astype(BF16)


def full_dispatch_kernel(scaled_ref, put_ref, out_ref):
    out_ref[...] = dot(put_ref[...], scaled_ref[...]).astype(BF16)


def full_spread_kernel(in_ref, out_ref, wide):
    for half in range(2):
        lanes = slice(half * 128, (half + 1) * 128)
        wide[half] = in_ref[:, lanes].astype(F32)
        for yc in range(YC):
            block = wide[half, pl.ds(yc, BLOCK, stride=YC)].astype(BF16)
            for x in range(X):
                out_ref[yc, x, :, lanes] = block


def spread_kernel(in_ref, out_ref, source_ref, wide):
    rows = in_ref[...]
    wide[...] = rows[:, 0:ROWS].astype(F32)
    lane = lax.broadcasted_iota(jnp.int32, (Z, ROWS), 1)
    counts = wide[pl.ds(SHORT - 1, Z, stride=SHORT)]
    crowded = jnp.max(jnp.where(lane == YC, counts, 0.0), axis=(0, 1), keepdims=True) > 0.5
    mark = jnp.where(crowded, jnp.inf, 0.0)
    counts = jnp.where(lane < YC, counts, 0.0).astype(BF16)
    lower = lax.broadcasted_iota(jnp.int32, (ROWS, ROWS), 0)
    upper = lax.broadcasted_iota(jnp.int32, (ROWS, ROWS), 1)
    starts = dot(counts, (lower < upper).astype(F32).astype(BF16)).astype(BF16)
    row = lax.broadcasted_iota(jnp.int32, (BLOCK, Z), 0)
    sender = (row // CAP == lax.broadcasted_iota(jnp.int32, (BLOCK, Z), 1)).astype(F32).astype(BF16)
    row = lax.broadcasted_iota(jnp.int32, (BLOCK, ROWS), 0)
    position = (row % CAP).astype(F32)
    source = (row // CAP * SHORT).astype(F32) + dot(sender, starts) + position
    source = jnp.where(position < dot(sender, counts), source, -1.0)
    rows_half, block_half = PACKED // 2, BLOCK // 2
    packed = lax.broadcasted_iota(jnp.int32, (block_half, rows_half), 1).astype(F32)
    for half in range(2):
        mine = pl.ds(half * block_half, block_half)
        wanted = source[half * block_half : (half + 1) * block_half] - float(half * rows_half)
        take = jnp.concatenate(
            [(packed == wanted[:, yc : yc + 1]).astype(F32).astype(BF16) for yc in range(YC)],
            axis=0,
        )
        blocks = dot(take, rows[half * rows_half : (half + 1) * rows_half])
        blocks = (blocks + mark).astype(BF16)
        for yc in range(YC):
            for x in range(X):
                out_ref[yc, x, mine] = blocks[yc * block_half : (yc + 1) * block_half]
    source = jnp.concatenate([source, jnp.full((ROWS - BLOCK, ROWS), -1.0, F32)], axis=0)
    source_ref[...] = jnp.transpose(source)[0:YC]


def expert_kernel(in_ref, gain_ref, up_ref, down_ref, out_ref, mark_ref):
    blocks = in_ref.shape[0]
    rows = jnp.concatenate(
        [in_ref[:, x].reshape(blocks * BLOCK, QUARTER) for x in range(X)], axis=1
    )
    centered = rows.astype(F32) * (1.0 / gain_ref[...])
    spread = jnp.sum(centered * centered, axis=1, keepdims=True) * (1.0 / WIDTH)
    marked = jnp.where(jnp.max(spread) == jnp.inf, 1, 0)

    @pl.when(pl.program_id(0) == 0)
    def _():
        mark_ref[0] = marked

    @pl.when(pl.program_id(0) > 0)
    def _():
        mark_ref[0] = jnp.maximum(mark_ref[0], marked)

    inverse = 1.0 / jnp.sqrt(spread + 1e-05)
    hidden = silu(dot(rows, up_ref[...]) * inverse).astype(BF16)
    result = dot(hidden, down_ref[...]).astype(BF16)
    for x in range(X):
        out_ref[:, x] = result[:, x * QUARTER : (x + 1) * QUARTER].reshape(blocks, BLOCK, QUARTER)


def experts(rows, gain, up, down):
    step = YC // 2
    return pl.pallas_call(
        expert_kernel,
        grid=(YC // step,),
        out_shape=(shape((YC, X, BLOCK, QUARTER), BF16), shape((1,), jnp.int32)),
        in_specs=[
            pl.BlockSpec((step, X, BLOCK, QUARTER), lambda i: (i, 0, 0, 0)),
            pl.BlockSpec((1, WIDTH), lambda i: (0, 0)),
            pl.BlockSpec((WIDTH, WIDTH), lambda i: (0, 0)),
            pl.BlockSpec((WIDTH, WIDTH), lambda i: (0, 0)),
        ],
        out_specs=(
            pl.BlockSpec((step, X, BLOCK, QUARTER), lambda i: (i, 0, 0, 0)),
            pl.BlockSpec(memory_space=pltpu.SMEM),
        ),
        cost_estimate=cost(4 * YC * BLOCK * WIDTH * WIDTH, 8 << 20),
        compiler_params=pltpu.CompilerParams(vmem_limit_bytes=40 << 20),
        name="experts",
    )(rows, gain, up, down)


def summed(in_ref, yc, lanes=slice(None)):
    total = in_ref[yc, 0, :, lanes].astype(F32)
    for x in range(1, X):
        total = total + in_ref[yc, x, :, lanes].astype(F32)
    return total


def full_collect_kernel(in_ref, out_ref, wide):
    for half in range(2):
        lanes = slice(half * 128, (half + 1) * 128)
        for yc in range(YC):
            wide[half, pl.ds(yc, BLOCK, stride=YC)] = summed(in_ref, yc, lanes)
        out_ref[:, lanes] = wide[half].astype(BF16)


def collect_kernel(in_ref, source_ref, out_ref):
    packed = lax.broadcasted_iota(jnp.int32, (PACKED, BLOCK), 0).astype(F32)
    result = jnp.zeros((PACKED, QUARTER), F32)
    for yc in range(YC):
        give = (packed == source_ref[yc : yc + 1, 0:BLOCK]).astype(F32).astype(BF16)
        result = result + dot(give, summed(in_ref, yc).astype(BF16))
    out_ref[...] = result.astype(BF16)


def combine_kernel(in_ref, pick_ref, gate_ref, mixed_ref, out_ref):
    rows = in_ref[...]
    moe = dot(pick_ref[0], rows) * gate_ref[0, :, 0:1]
    moe = moe + dot(pick_ref[1], rows) * gate_ref[1, :, 0:1]
    out_ref[...] = (mixed_ref[...] + moe).astype(BF16)


def exchange(value, axes):
    return lax.all_to_all(value, axes, split_axis=0, concat_axis=0, tiled=True)


def through_experts(rows, gain, w_up, w_down):
    rows = exchange(rows.reshape(YC * X, BLOCK, QUARTER), ("y", "c", "x"))
    rows, marked = experts(rows.reshape(YC, X, BLOCK, QUARTER), gain, w_up[0], w_down[0])
    rows = exchange(rows.reshape(YC * X, BLOCK, QUARTER), ("y", "c", "x"))
    return rows.reshape(YC, X, BLOCK, QUARTER), marked


def on_device(
    glu, dw_kernel, bn_scale, bn_shift, pw_out, block_input, ln_gain, w_up, w_down, routes, gates
):
    seq = ("z", "y", "c")
    count = Z * Y * C
    pairs = [(i, i + 1) for i in range(1, count - 1, 2)]
    beyond = lax.ppermute(glu, seq, pairs + [(j, i) for i, j in pairs])
    own = call(
        own_conv_kernel,
        shape((ROWS, QUARTER), F32),
        "own_conv",
        vmem=60 << 20,
        scratch=[pltpu.VMEM((ROWS + 2 * EDGE, QUARTER), F32)],
    )(glu, dw_kernel)
    core = lax.axis_index("c").astype(jnp.int32).reshape(1)
    edge = call(edge_kernel, shape((EDGE, QUARTER), BF16), "edge", vmem=60 << 20, smem=(0,))(core, glu)
    pairs = [(i, i + 1) for i in range(0, count, 2)]
    beside = lax.ppermute(edge, seq, pairs + [(j, i) for i, j in pairs])
    gain = ln_gain.reshape(1, WIDTH)
    hid_index = lax.axis_index("x").astype(jnp.int32).reshape(1)

    put, counts, pick, gate = call(
        routing_kernel,
        (
            shape((PACKED, ROWS), BF16),
            shape((PACKED, ROWS), BF16),
            shape((2, ROWS, PACKED), BF16),
            shape((2, ROWS, ROWS), F32),
        ),
        "routing",
    )(routes.T, gates.T)
    parts = call(
        front_kernel,
        shape((X, ROWS + AUX, QUARTER), BF16),
        "front",
        vmem=60 << 20,
        smem=(0,),
        scratch=[
            pltpu.VMEM((3 * EDGE, QUARTER), F32),
            pltpu.VMEM((3 * EDGE, QUARTER), F32),
            pltpu.VMEM((ROWS, QUARTER), F32),
        ],
    )(
        core,
        own,
        beyond,
        beside,
        dw_kernel,
        bn_scale.reshape(1, QUARTER),
        bn_shift.reshape(1, QUARTER),
        pw_out,
        block_input,
    )
    parts = exchange(parts, "x")
    mixed, scaled, rows = call(
        dispatch_kernel,
        (
            shape((ROWS, QUARTER), F32),
            shape((ROWS, QUARTER), BF16),
            shape((PACKED, QUARTER), BF16),
        ),
        "dispatch",
        smem=(0,),
    )(hid_index, parts, block_input, gain, put, counts)
    rows = exchange(rows, "z")
    rows, source = call(
        spread_kernel,
        (shape((YC, X, BLOCK, QUARTER), BF16), shape((YC, ROWS), F32)),
        "spread",
        scratch=[pltpu.VMEM((PACKED, ROWS), F32)],
    )(rows)
    rows, marked = through_experts(rows, gain, w_up, w_down)
    rows = call(collect_kernel, shape((PACKED, QUARTER), BF16), "collect")(rows, source)
    rows = exchange(rows, "z")

    def short(rows):
        return call(combine_kernel, shape((ROWS, QUARTER), BF16), "combine")(
            rows, pick, gate, mixed
        )

    def full(_):
        put, pick = call(
            full_routing_kernel,
            (shape((SLOTS, ROWS), BF16), shape((2, ROWS, SLOTS), BF16)),
            "full_routing",
        )(routes.T)
        rows = call(full_dispatch_kernel, shape((SLOTS, QUARTER), BF16), "full_dispatch")(scaled, put)
        rows = call(
            full_spread_kernel,
            shape((YC, X, BLOCK, QUARTER), BF16),
            "full_spread",
            scratch=[pltpu.VMEM((2, SLOTS, 128), F32)],
        )(exchange(rows, "z"))
        rows, _ = through_experts(rows, gain, w_up, w_down)
        rows = call(
            full_collect_kernel,
            shape((SLOTS, QUARTER), BF16),
            "full_collect",
            scratch=[pltpu.VMEM((2, SLOTS, 128), F32)],
        )(rows)
        return call(combine_kernel, shape((ROWS, QUARTER), BF16), "full_combine")(
            exchange(rows, "z"), pick, gate, mixed
        )

    return lax.cond(marked[0] > 0, full, short, rows)


def solution(mesh):
    chips = Mesh(mesh.devices.reshape(Z, Y, C, X), ("z", "y", "c", "x"))
    seq = ("z", "y", "c")
    in_specs = (
        P(seq, "x"),
        P(None, "x"),
        P("x"),
        P("x"),
        P("x", None),
        P(seq, None),
        P(),
        P(seq, None, "x"),
        P(seq, "x", None),
        P(seq, None),
        P(seq, None),
    )
    return jax.shard_map(
        on_device, mesh=chips, in_specs=in_specs, out_specs=P(seq, "x"), check_vma=False
    )
```
